256 devices in a mesh: dp: 4 (over x), head: 4 (over y), ctx: 16 (over z, core).
Axes of the slice: x: 4, y: 4, z: 8, core: 2. Of those that a mesh axis runs over, the one named last changes fastest.
Arguments:
- q_count: int32 [4, 8192, 3584], P('dp', 'ctx', 'head'), may hold values from 0 to 4
- k_count: int32 [4, 8192, 3584], P('dp', 'ctx', 'head'), may hold values from 0 to 4
- v_count: int32 [4, 8192, 3584], P('dp', 'ctx', 'head'), may hold values from 0 to 4
- q_pre: bfloat16 [4, 8192, 3584], P('dp', 'ctx', 'head'), may hold values from -6 to 6
- k_pre: bfloat16 [4, 8192, 3584], P('dp', 'ctx', 'head'), may hold values from -6 to 6
- v_pre: bfloat16 [4, 8192, 3584], P('dp', 'ctx', 'head'), may hold values from -6 to 6
- grad_y: bfloat16 [4, 8192, 3584], P('dp', 'ctx', 'head'), may hold values from -6 to 6
- gain: float32 [3584], P('head'), may hold values from 0.25 to 1.75
Outputs:
- grad_q_pre: bfloat16 [4, 8192, 3584], P('dp', 'ctx', 'head')
- grad_k_pre: bfloat16 [4, 8192, 3584], P('dp', 'ctx', 'head')
- grad_v_pre: bfloat16 [4, 8192, 3584], P('dp', 'ctx', 'head')
- grad_gain: float32 [3584], P('head')
The draws below stay inside these ranges and needn't reach their ends.
Inputs may be any that keep to these rules, and one draw needn't show every extreme that they name: `q_count`: each count is how many of the 4 steps fired. `k_count`: each count is how many of the 4 steps fired. `v_count`: each count is how many of the 4 steps fired.
All inputs are finite; a program needn't handle non-finite values.
Results may differ from the reference program's by a relative error of at most 0.001.
Values sent between devices are 32-bit elements; how exact they have to be, the bound alone decides.
No kernel may reach another device: no remote copies, remote signals or barrier semaphores. Data moves between devices by JAX's collectives and lax.ppermute only.
A program may use at most 128 MiB of HBM per device.

```python
import math
import jax
import jax.numpy as jnp
from jax import lax

HEADS = 28
E = 128
SPIKE_STEPS = 4
SEQS = 4
LENGTH = 8192
CHANNELS = 3584


def touch_ends(values, own_key, smallest, high):
    place = [jax.random.randint(jax.random.fold_in(own_key, axis), (), 0, length) for axis, length in enumerate(values.shape)]
    longest = values.shape.index(max(values.shape))
    next_to = place[:longest] + [(place[longest] + 1) % values.shape[longest]] + place[longest + 1:]
    return values.at[tuple(place)].set(smallest).at[tuple(next_to)].set(high)


def shard_levels(key, extent, split, low, top_value):
    level, own = 1.0, jax.random.fold_in(key, 6)
    for dim, shards_of in split:
        draws = jnp.exp(jax.random.uniform(jax.random.fold_in(own, dim), (shards_of,), jnp.float32, low / len(split), top_value / len(split)))
        level = level * jnp.repeat(draws, extent[dim] // shards_of).reshape([-1 if axis == dim else 1 for axis in range(len(extent))])
    return level


def bell_draw(stream_key, extent, spread, limit, split=(), kind=jnp.bfloat16):
    entries = spread * jax.random.normal(stream_key, extent, jnp.float32)
    if split:
        entries = entries * shard_levels(stream_key, extent, split, -0.22, 0.18)
    return jnp.clip(entries, -limit, limit).astype(kind)


def setup_inputs(seed: int = 0) -> dict:
    key_list = jax.random.split(jax.random.key(seed), 9)
    return {
        "q_count": touch_ends(jax.random.randint(key_list[0], (SEQS, LENGTH, CHANNELS), 0, SPIKE_STEPS + 1), jax.random.fold_in(key_list[0], 1), 0, SPIKE_STEPS).astype(jnp.int32),
        "k_count": touch_ends(jax.random.randint(key_list[1], (SEQS, LENGTH, CHANNELS), 0, SPIKE_STEPS + 1), jax.random.fold_in(key_list[1], 1), 0, SPIKE_STEPS).astype(jnp.int32),
        "v_count": touch_ends(jax.random.randint(key_list[2], (SEQS, LENGTH, CHANNELS), 0, SPIKE_STEPS + 1), jax.random.fold_in(key_list[2], 1), 0, SPIKE_STEPS).astype(jnp.int32),
        "q_pre": bell_draw(key_list[3], (SEQS, LENGTH, CHANNELS), 1.0, 6.0, ((0, 4), (1, 16), (2, 4))),
        "k_pre": bell_draw(key_list[4], (SEQS, LENGTH, CHANNELS), 1.0, 6.0, ((0, 4), (1, 16), (2, 4))),
        "v_pre": bell_draw(key_list[5], (SEQS, LENGTH, CHANNELS), 1.0, 6.0, ((0, 4), (1, 16), (2, 4))),
        "grad_y": bell_draw(key_list[6], (SEQS, LENGTH, CHANNELS), 1.0, 6.0, ((0, 4), (1, 16), (2, 4))),
        "gain": jnp.clip(1.0 + 0.15 * jax.random.normal(key_list[7], (CHANNELS,), jnp.float32), 0.25, 1.75),
    }


HIGHEST = lax.Precision.HIGHEST

def spike_values(count):
    return (count.astype(jnp.float32) - SPIKE_STEPS / 2) * 0.5

def surrogate(pre):
    value = pre.astype(jnp.float32)
    total = jnp.zeros_like(value)
    for level in range(SPIKE_STEPS):
        switch = jax.nn.sigmoid(4.0 * (value - level + (SPIKE_STEPS - 1) / 2))
        total = total + 2.0 * switch * (1.0 - switch)
    return total

def one_sequence(q_count, k_count, v_count, q_pre, k_pre, v_pre, grad_y, gain_head):
    length = q_count.shape[0]
    block = min(512, length)
    blocks = length // block
    factor = 1.0 / math.sqrt(E * length)
    q_spike = spike_values(q_count).reshape(blocks, block, E)
    k_spike = spike_values(k_count).reshape(blocks, block, E)
    v_spike = spike_values(v_count).reshape(blocks, block, E)
    q_short = q_spike.astype(jnp.bfloat16)
    k_short = k_spike.astype(jnp.bfloat16)
    v_short = v_spike.astype(jnp.bfloat16)
    grad_in = grad_y.astype(jnp.float32).reshape(blocks, block, E)
    grad_out = grad_in * gain_head
    kv_blocks = jnp.einsum('nre,nrf->nef', k_short, v_short, preferred_element_type=jnp.float32)
    qd_blocks = factor * jnp.einsum('nre,nrf->nef', q_spike, grad_out, precision=HIGHEST)
    state_prev = jnp.cumsum(kv_blocks, 0) - kv_blocks
    grad_next = lax.optimization_barrier(jnp.sum(qd_blocks, 0))[None] - jnp.cumsum(qd_blocks, 0)
    causal = (lax.broadcasted_iota(jnp.int32, (block, block), 0) >= lax.broadcasted_iota(jnp.int32, (block, block), 1)).astype(jnp.float32)
    scores = jnp.einsum('nre,nse->nrs', q_short, k_short, preferred_element_type=jnp.float32) * causal
    weights = jnp.einsum('nrf,nsf->nrs', grad_out, v_spike, precision=HIGHEST) * causal
    out = factor * (jnp.einsum('nrs,nsf->nrf', scores, v_spike, precision=HIGHEST) + jnp.einsum('nre,nef->nrf', q_spike, state_prev, precision=HIGHEST))
    dq_spike = factor * (jnp.einsum('nrs,nse->nre', weights, k_spike, precision=HIGHEST) + jnp.einsum('nrf,nef->nre', grad_out, state_prev, precision=HIGHEST))
    dk_spike = factor * jnp.einsum('nrs,nre->nse', weights, q_spike, precision=HIGHEST) + jnp.einsum('nrf,nef->nre', v_spike, grad_next, precision=HIGHEST)
    dv_spike = factor * jnp.einsum('nrs,nrf->nsf', scores, grad_out, precision=HIGHEST) + jnp.einsum('nre,nef->nrf', k_spike, grad_next, precision=HIGHEST)
    gain_part = lax.optimization_barrier(jnp.sum(out * grad_in, axis=(0, 1)))
    grad_q = (dq_spike.reshape(length, E) * surrogate(q_pre)).astype(jnp.bfloat16)
    grad_k = (dk_spike.reshape(length, E) * surrogate(k_pre)).astype(jnp.bfloat16)
    grad_v = (dv_spike.reshape(length, E) * surrogate(v_pre)).astype(jnp.bfloat16)
    return (grad_q, grad_k, grad_v, gain_part)

def reference(q_count, k_count, v_count, q_pre, k_pre, v_pre, grad_y, gain):

    def per_head(head):
        start = head * E

        def take(array):
            return lax.dynamic_slice_in_dim(array, start, E, 2)
        gain_head = lax.dynamic_slice_in_dim(gain, start, E, 0)
        grad_q, grad_k, grad_v, gain_part = jax.vmap(one_sequence, in_axes=(0, 0, 0, 0, 0, 0, 0, None))(take(q_count), take(k_count), take(v_count), take(q_pre), take(k_pre), take(v_pre), take(grad_y), gain_head)
        return (grad_q, grad_k, grad_v, lax.optimization_barrier(jnp.sum(gain_part, 0)))
    head_index = jnp.arange(HEADS, dtype=jnp.int32)
    grad_q, grad_k, grad_v, grad_gain = lax.map(per_head, head_index)

    def assemble(stack):
        return jnp.transpose(stack, (1, 2, 0, 3)).reshape(SEQS, LENGTH, HEADS * E)
    return (assemble(grad_q), assemble(grad_k), assemble(grad_v), grad_gain.reshape(HEADS * E))
```

```python
import math

import jax
import jax.numpy as jnp
from jax import lax
from jax.experimental import pallas as pl
from jax.experimental.pallas import tpu as pltpu
from jax.sharding import PartitionSpec as P

E = 128
SPIKE_STEPS = 4
F32 = jnp.float32
BF16 = jnp.bfloat16
UNIT = 8
CHUNK = 128


def spike(count):
    return ((count.astype(F32) - SPIKE_STEPS / 2) * 0.5).astype(BF16)


def mm(a, b, ca, cb):
    return lax.dot_general(a, b, (((ca,), (cb,)), ((), ())), preferred_element_type=F32)


def halves(x):
    hi = x.astype(BF16)
    return hi, (x - hi.astype(F32)).astype(BF16)


def surrogate(pre):
    w = pre.astype(F32) * (4.0 / math.log(2.0))
    c = jnp.exp2(w) + jnp.exp2(-w)
    b1, b2 = 2.0 * math.cosh(2.0), 2.0 * math.cosh(6.0)
    below = (c + b1) * (c + b2)
    r = pl.reciprocal(below, approx=True)
    r = r * (2.0 - below * r)
    n3 = 2.0 * (b1 + b2)
    n2 = 16.0 + 8.0 * b1 * b2
    n1 = 16.0 * (b1 + b2) + 2.0 * b1 * b2 * (b1 + b2)
    n0 = 8.0 * (b1 * b1 + b2 * b2)
    above = ((n3 * c + n2) * c + n1) * c + n0
    return (above * r) * r


def place():
    me = lax.axis_index("ctx")
    chip, core = me // 2, lax.rem(me, 2)
    return chip, core, 1 - 2 * core


def around(chip, steps, chips):
    return lax.rem(chip + steps + chips, chips)


def unit_list(chip, core, way, chips):
    units = []
    for k in range(1, chips // 2):
        shard = around(chip, way * k, chips)
        units += [2 * shard, 2 * shard + 1]
    return units + [2 * around(chip, chips // 2, chips) + core, 2 * chip + core]


def rows_of(unit):
    return pl.ds(pl.multiple_of(unit * UNIT, UNIT), UNIT)


def states_body(
    chips, heads, factor, q_ref, k_ref, v_ref, gy_ref,
    keep_ref, send_ref, qs_ref, ks_ref, vs_ref, gy_out, counts, both, sems,
):
    chip, core, way = place()
    mine = unit_list(chip, core, way, chips)
    other = unit_list(chip, 1 - core, -way, chips)
    copies = []
    for h in range(heads):
        lanes = slice(h * E, (h + 1) * E)
        pairs = [(ref.at[0, :, lanes], counts.at[i, :, lanes]) for i, ref in enumerate((q_ref, k_ref, v_ref))]
        pairs.append((gy_ref.at[0, :, lanes], gy_out.at[:, lanes]))
        copies.append([pltpu.make_async_copy(a, b, sems.at[i, h]) for i, (a, b) in enumerate(pairs)])
        for copy in copies[-1]:
            copy.start()
    for h in range(heads):
        lanes = slice(h * E, (h + 1) * E)
        for copy in copies[h]:
            copy.wait()
        q, k, v = (spike(counts[i, :, lanes]) for i in range(3))
        qs_ref[:, lanes] = q
        ks_ref[:, lanes] = k
        vs_ref[:, lanes] = v
        both[0, h] = mm(k, v, 0, 0)
        both[1, h] = factor * mm(q, gy_out[:, lanes], 0, 0)
    for i, (here, there) in enumerate(zip(mine, other)):
        for t in range(2):
            keep_ref[2 * i + t] = both[t, :, rows_of(here)]
            send_ref[2 * i + t] = both[t, :, rows_of(there)]
        send_ref[2 * len(mine) + i] = both[core, :, rows_of(here)]


def chip_body(chips, heads, keep_ref, got_ref, m1_ref, m2_ref, m3_ref, m4_ref, own_ref, g_ref):
    core = lax.rem(lax.axis_index("ctx"), 2)
    targets = [(m1_ref, 0), (m1_ref, 1), (m2_ref, 0), (m2_ref, 1), (m3_ref, 0), (m3_ref, 1)]
    targets += [(m4_ref, 0), (own_ref, 0)]
    cross = jnp.zeros((heads, UNIT, E), F32)
    for i, (ref, at) in enumerate(targets):
        kv, qd = keep_ref[2 * i], keep_ref[2 * i + 1]
        kv_got, qd_got = got_ref[2 * i], got_ref[2 * i + 1]
        ref[2 * at * heads : (2 * at + 1) * heads] = kv + kv_got
        ref[(2 * at + 1) * heads : (2 * at + 2) * heads] = qd + qd_got
        cross = cross + jnp.where(core == 0, kv * qd_got, kv_got * qd)
    g_ref[0] = jnp.zeros((UNIT, E), F32)
    g_ref[0, 0:heads] = jnp.sum(cross, axis=1)


def scan_body(chips, heads, x_ref, y_ref, o1_ref, o2_ref, o3_ref, o4_ref, own_ref, g_ref, have, give):
    chip, core, way = place()
    wide, near = 4 * heads, chips // 2
    for ref, go, lane in ((x_ref, way, core), (y_ref, -way, 1 - core)):
        for k in range(1, near):
            at = around(chip, -go * k, chips)
            have[at] = ref[wide * (k - 1) : wide * k].reshape(2, 2 * heads, UNIT, E)
        base = wide * (near - 1)
        have[around(chip, near, chips), lane] = ref[base : base + 2 * heads]
        have[chip, lane] = ref[base + 2 * heads : base + 4 * heads]
    zero = jnp.zeros((2, heads, UNIT, E), F32)
    before, after, cross = zero, zero, zero
    for i in range(chips):
        give[i, :, 0:heads] = before
        cross = cross + before * have[i, :, heads : 2 * heads]
        before = before + have[i, :, 0:heads]
    for i in reversed(range(chips)):
        give[i, :, heads : 2 * heads] = after
        after = after + have[i, :, heads : 2 * heads]
    last = wide * near
    g_ref[...] = x_ref[last : last + 1] + y_ref[last : last + 1]
    g_ref[0, 0:heads] = g_ref[0, 0:heads] + jnp.sum(cross[0] + cross[1], axis=1)
    for k, ref in ((1, o1_ref), (2, o2_ref), (3, o3_ref)):
        ref[0:wide] = give[around(chip, way * k, chips)].reshape(wide, UNIT, E)
        ref[wide : wide + 1] = g_ref[...]
    o4_ref[0 : 2 * heads] = give[around(chip, near, chips), core]
    o4_ref[2 * heads : 2 * heads + 1] = g_ref[...]
    own_ref[...] = give[chip].reshape(wide, UNIT, E)


def intra_body(heads, factor, qs_ref, ks_ref, vs_ref, gy_ref, gain_ref, dq_ref, dk_ref, dv_ref, g_ref):
    count = qs_ref.shape[0] // CHUNK
    first = lax.broadcasted_iota(jnp.int32, (CHUNK, CHUNK), 0)
    second = lax.broadcasted_iota(jnp.int32, (CHUNK, CHUNK), 1)
    lower, upper = first >= second, first <= second

    def twice(x, axis=1):
        return jnp.concatenate([x, x], axis=axis)

    def per_head(h, carry):
        lanes = pl.ds(pl.multiple_of(h * E, E), E)
        at = [slice(i * CHUNK, (i + 1) * CHUNK) for i in range(count)]
        q, k, v, gy = ([ref[rows, lanes] for rows in at] for ref in (qs_ref, ks_ref, vs_ref, gy_ref))
        gain = gain_ref[h]
        g_hi, g_lo = halves(gain)
        dq, dk, dv = [], [], []
        for i in range(count):
            vg = jnp.concatenate([v[i] * g_hi, v[i] * g_lo], axis=1)
            weights = jnp.where(lower, mm(twice(gy[i]), vg, 1, 1), 0.0)
            w_hi, w_lo = halves(weights)
            dq.append(mm(jnp.concatenate([w_hi, w_lo], axis=1), twice(k[i], 0), 1, 0))
            dk.append(mm(jnp.concatenate([w_hi, w_lo], axis=0), twice(q[i], 0), 0, 0))
            s_hi, s_lo = halves(jnp.where(upper, mm(k[i], q[i], 1, 1), 0.0))
            dv.append(mm(jnp.concatenate([s_hi, s_lo], axis=1), twice(gy[i], 0), 1, 0))
        state = None
        for i in range(count):
            if i > 0:
                kv = mm(k[i - 1], v[i - 1], 0, 0)
                state = kv if state is None else state + kv
                dq[i] += mm(twice(gy[i]), jnp.concatenate(halves(state * gain), axis=1), 1, 1)
            dq_ref[at[i], lanes] = factor * dq[i]
        state = None
        total = jnp.zeros((1, E), F32)
        for i in reversed(range(count)):
            if i + 1 < count:
                qd = mm(q[i + 1], gy[i + 1], 0, 0)
                state = qd if state is None else state + qd
                dk[i] += mm(twice(v[i]), jnp.concatenate(halves(state * gain), axis=1), 1, 1)
                dv[i] += mm(twice(k[i]), jnp.concatenate(halves(state), axis=0), 1, 0)
            dk_ref[at[i], lanes] = factor * dk[i]
            dv_plain = factor * dv[i]
            dv_ref[at[i], lanes] = dv_plain * gain
            total = total + jnp.sum(v[i].astype(F32) * dv_plain, axis=0, keepdims=True)
        g_ref[h] = total
        return carry

    lax.fori_loop(0, heads, per_head, 0)


def slope_body(q_ref, k_ref, v_ref, sq_ref, sk_ref, sv_ref):
    step = 32

    def some_rows(i, carry):
        rows = pl.ds(pl.multiple_of(i * step, step), step)
        for pre, out in ((q_ref, sq_ref), (k_ref, sk_ref), (v_ref, sv_ref)):
            out[rows] = surrogate(pre[0, rows])
        return carry

    lax.fori_loop(0, q_ref.shape[1] // step, some_rows, 0)


def finish_body(
    chips, heads, factor, u_ref, w_ref, own_ref, got_ref, gain_ref, gy_ref, ks_ref, vs_ref,
    dq_ref, dk_ref, dv_ref, sq_ref, sk_ref, sv_ref, oq_ref, ok_ref, ov_ref,
    state, stage, sems,
):
    chip, core, way = place()
    wide, near = 4 * heads, chips // 2
    tiles = wide + 1
    for ref, go, lane in ((u_ref, way, core), (w_ref, -way, 1 - core)):
        for k in range(1, near):
            shard = around(chip, -go * k, chips)
            for b in range(2):
                for t in range(2):
                    base = tiles * (k - 1) + (2 * b + t) * heads
                    state[t, :, rows_of(2 * shard + b)] = ref[base : base + heads]
        for t in range(2):
            base = tiles * (near - 1) + t * heads
            unit = 2 * around(chip, near, chips) + lane
            state[t, :, rows_of(unit)] = ref[base : base + heads]
    for b in range(2):
        for t in range(2):
            base = (2 * b + t) * heads
            state[t, :, rows_of(2 * chip + b)] = own_ref[base : base + heads]
    kind = 1 - core
    mine = unit_list(chip, core, way, chips)
    other = unit_list(chip, 1 - core, -way, chips)
    for i, (here, there) in enumerate(zip(mine, other)):
        state[kind, :, rows_of(here)] += got_ref[2 * i + kind]
        state[kind, :, rows_of(there)] += got_ref[2 * len(mine) + i]
    copies = []
    for h in range(heads):
        lanes = slice(h * E, (h + 1) * E)
        gain = gain_ref[h]
        gy, k, v = gy_ref[:, lanes], ks_ref[:, lanes], vs_ref[:, lanes]
        m2 = jnp.concatenate(halves(state[0, h] * (gain * factor)), axis=1)
        g_hi, g_lo = halves(state[1, h] * gain)
        dq = dq_ref[:, lanes] + mm(jnp.concatenate([gy, gy], axis=1), m2, 1, 1)
        stage[0, :, lanes] = (dq * sq_ref[:, lanes]).astype(BF16)
        dk = dk_ref[:, lanes] + mm(
            jnp.concatenate([v, v], axis=1), jnp.concatenate([g_hi, g_lo], axis=1), 1, 1
        )
        stage[1, :, lanes] = (dk * sk_ref[:, lanes]).astype(BF16)
        dv = dv_ref[:, lanes] + mm(
            jnp.concatenate([k, k], axis=1), jnp.concatenate([g_hi, g_lo], axis=0), 1, 0
        )
        stage[2, :, lanes] = (dv * sv_ref[:, lanes]).astype(BF16)
        for i, out in enumerate((oq_ref, ok_ref, ov_ref)):
            copy = pltpu.make_async_copy(stage.at[i, :, lanes], out.at[0, :, lanes], sems.at[i, h])
            copy.start()
            copies.append(copy)
    for copy in copies:
        copy.wait()


def params(mib, **more):
    return pltpu.CompilerParams(vmem_limit_bytes=mib * 1024 * 1024, **more)


def cost(us):
    return pl.CostEstimate(flops=int(us * 1e9), bytes_accessed=int(us * 2e6), transcendentals=0)


def per_device(q_count, k_count, v_count, q_pre, k_pre, v_pre, grad_y, gain):
    rows, width = q_count.shape[1], q_count.shape[2]
    heads = width // E
    devices = lax.axis_size("ctx")
    chips = devices // 2
    near = chips // 2
    factor = 1.0 / math.sqrt(E * rows * devices)
    units = E // UNIT
    assert units == devices and near == 4
    gain_h = gain.reshape(heads, 1, E)

    def shape(*dims, dtype=F32):
        return jax.ShapeDtypeStruct(dims, dtype)

    def tiles(count):
        return shape(count, UNIT, E)

    swap = [(i, i ^ 1) for i in range(devices)]

    def ring(k):
        pairs = []
        for z in range(chips):
            pairs.append((2 * z, 2 * ((z + k) % chips)))
            pairs.append((2 * z + 1, 2 * ((z - k) % chips) + 1))
        return pairs

    def exchange(parts):
        return [lax.ppermute(part, "ctx", ring(k)) for k, part in enumerate(parts, 1)]

    with jax.named_scope("local_states"):
        keep, send, q_spike, k_spike, v_spike, gy = pl.pallas_call(
            lambda *refs: states_body(chips, heads, factor, *refs),
            in_specs=[pl.BlockSpec(memory_space=pltpu.HBM)] * 4,
            out_shape=[shape(units, heads, UNIT, E), shape(units * 3 // 2, heads, UNIT, E)]
            + [shape(rows, width, dtype=BF16)] * 4,
            scratch_shapes=[
                pltpu.VMEM((3, rows, width), jnp.int32),
                pltpu.VMEM((2, heads, E, E), F32),
                pltpu.SemaphoreType.DMA((4, heads)),
            ],
            compiler_params=params(9),
            cost_estimate=cost(3),
            name="local_states",
        )(*(pltpu.with_memory_space_constraint(x, pltpu.HBM) for x in (q_count, k_count, v_count, grad_y)))
        got = lax.ppermute(send, "ctx", swap)

    with jax.named_scope("chip_states"):
        *parts, own, g_chip = pl.pallas_call(
            lambda *refs: chip_body(chips, heads, *refs),
            out_shape=[tiles(4 * heads)] * 3 + [tiles(2 * heads)] * 2 + [tiles(1)],
            compiler_params=params(2),
            name="chip_states",
        )(keep, got)

    with jax.named_scope("to_owners"):
        parts = exchange(parts)

    with jax.named_scope("intra"):
        gain_late, parts[0] = lax.optimization_barrier((gain_h, parts[0]))
        dq, dk, dv, g_intra = pl.pallas_call(
            lambda *refs: intra_body(heads, factor, *refs),
            out_shape=[shape(rows, width)] * 3 + [shape(heads, 1, E)],
            compiler_params=params(4),
            cost_estimate=cost(7),
            name="intra",
        )(q_spike, k_spike, v_spike, gy, gain_late)

    with jax.named_scope("to_core"):
        g_mine = g_chip + jnp.pad(g_intra.reshape(1, heads, E), ((0, 0), (0, UNIT - heads), (0, 0)))
        pack = jnp.concatenate([*parts, own, g_mine])
        pack_got = lax.ppermute(pack, "ctx", swap)

    with jax.named_scope("scan"):
        *parts, own, g_all = pl.pallas_call(
            lambda *refs: scan_body(chips, heads, *refs),
            out_shape=[tiles(4 * heads + 1)] * 3 + [tiles(2 * heads + 1), tiles(4 * heads), tiles(1)],
            scratch_shapes=[pltpu.VMEM((chips, 2, 2 * heads, UNIT, E), F32)] * 2,
            compiler_params=params(4),
            name="scan",
        )(pack, pack_got)

    with jax.named_scope("from_owners"):
        parts = exchange(parts)

    with jax.named_scope("slopes"):
        *late, parts[0] = lax.optimization_barrier((q_pre, k_pre, v_pre, parts[0]))
        sq, sk, sv = pl.pallas_call(
            slope_body,
            out_shape=[shape(rows, width)] * 3,
            compiler_params=params(2),
            cost_estimate=cost(5),
            name="slopes",
        )(*late)

    with jax.named_scope("states"):
        sq, *parts = lax.optimization_barrier((sq, *parts))
        mine = jnp.concatenate(parts)
        theirs = lax.ppermute(mine, "ctx", swap)

    with jax.named_scope("grad_gain"):
        lasts = [(4 * heads + 1) * (i + 1) - 1 for i in range(near - 1)]
        g_sum = g_all + mine[-1:]
        for i in lasts:
            g_sum = g_sum + mine[i : i + 1] + theirs[i : i + 1]
        size = lax.axis_size("dp")
        total = g_sum
        for step in range(1, size):
            total = total + lax.ppermute(
                g_sum, "dp", [(i, (i + step) % size) for i in range(size)]
            )
        grad_gain = total[0, :heads].reshape(width)

    with jax.named_scope("finish"):
        whole = pl.BlockSpec(memory_space=pltpu.VMEM)
        grads = pl.pallas_call(
            lambda *refs: finish_body(chips, heads, factor, *refs),
            in_specs=[whole] * 14,
            out_specs=[pl.BlockSpec(memory_space=pl.ANY)] * 3,
            out_shape=[shape(1, rows, width, dtype=BF16)] * 3,
            scratch_shapes=[
                pltpu.VMEM((2, heads, E, E), F32),
                pltpu.VMEM((3, rows, width), BF16),
                pltpu.SemaphoreType.DMA((3, heads)),
            ],
            compiler_params=params(8),
            name="finish",
        )(mine, theirs, own, got, gain_h, gy, k_spike, v_spike, dq, dk, dv, sq, sk, sv)
    return (*grads, grad_gain)


def solution(mesh):
    placed = P("dp", "ctx", "head")
    return jax.shard_map(
        per_device,
        mesh=mesh,
        in_specs=(placed,) * 7 + (P("head"),),
        out_specs=(placed,) * 3 + (P("head"),),
        check_vma=False,
    )
```

```python
import math

import jax
import jax.numpy as jnp
from jax import lax
from jax.experimental import pallas as pl
from jax.experimental.pallas import tpu as pltpu
from jax.sharding import PartitionSpec as P

E = 128
SPIKE_STEPS = 4
F32 = jnp.float32
BF16 = jnp.bfloat16
UNIT = 8
CHUNK = 128


def spike(count):
    return ((count.astype(F32) - SPIKE_STEPS / 2) * 0.5).astype(BF16)


def mm(a, b, ca, cb):
    return lax.dot_general(a, b, (((ca,), (cb,)), ((), ())), preferred_element_type=F32)


def halves(x):
    hi = x.astype(BF16)
    return hi, (x - hi.astype(F32)).astype(BF16)


def surrogate(pre):
    w = pre.astype(F32) * (4.0 / math.log(2.0))
    c = jnp.exp2(w) + jnp.exp2(-w)
    b1, b2 = 2.0 * math.cosh(2.0), 2.0 * math.cosh(6.0)
    below = (c + b1) * (c + b2)
    r = pl.reciprocal(below, approx=True)
    r = r * (2.0 - below * r)
    n3 = 2.0 * (b1 + b2)
    n2 = 16.0 + 8.0 * b1 * b2
    n1 = 16.0 * (b1 + b2) + 2.0 * b1 * b2 * (b1 + b2)
    n0 = 8.0 * (b1 * b1 + b2 * b2)
    above = ((n3 * c + n2) * c + n1) * c + n0
    return (above * r) * r


def place():
    me = lax.axis_index("ctx")
    chip, core = me // 2, lax.rem(me, 2)
    return chip, core, 1 - 2 * core


def around(chip, steps, chips):
    return lax.rem(chip + steps + chips, chips)


def unit_list(chip, core, way, chips):
    units = []
    for k in range(1, chips // 2):
        shard = around(chip, way * k, chips)
        units += [2 * shard, 2 * shard + 1]
    return units + [2 * around(chip, chips // 2, chips) + core, 2 * chip + core]


def rows_of(unit):
    return pl.ds(pl.multiple_of(unit * UNIT, UNIT), UNIT)


def states_body(
    chips, heads, factor, q_ref, k_ref, v_ref, gy_ref,
    keep_ref, send_ref, qs_ref, ks_ref, vs_ref, gy_out, counts, both, sems,
):
    chip, core, way = place()
    mine = unit_list(chip, core, way, chips)
    other = unit_list(chip, 1 - core, -way, chips)
    copies = []
    for h in range(heads):
        lanes = slice(h * E, (h + 1) * E)
        pairs = [(ref.at[0, :, lanes], counts.at[i, :, lanes]) for i, ref in enumerate((q_ref, k_ref, v_ref))]
        pairs.append((gy_ref.at[0, :, lanes], gy_out.at[:, lanes]))
        copies.append([pltpu.make_async_copy(a, b, sems.at[i, h]) for i, (a, b) in enumerate(pairs)])
        for copy in copies[-1]:
            copy.start()
    for h in range(heads):
        lanes = slice(h * E, (h + 1) * E)
        for copy in copies[h]:
            copy.wait()
        q, k, v = (spike(counts[i, :, lanes]) for i in range(3))
        qs_ref[:, lanes] = q
        ks_ref[:, lanes] = k
        vs_ref[:, lanes] = v
        both[0, h] = mm(k, v, 0, 0)
        both[1, h] = factor * mm(q, gy_out[:, lanes], 0, 0)
    for i, (here, there) in enumerate(zip(mine, other)):
        for t in range(2):
            keep_ref[2 * i + t] = both[t, :, rows_of(here)]
            send_ref[2 * i + t] = both[t, :, rows_of(there)]
        send_ref[2 * len(mine) + i] = both[core, :, rows_of(here)]


def chip_body(chips, heads, keep_ref, got_ref, m1_ref, m2_ref, m3_ref, m4_ref, own_ref, g_ref):
    core = lax.rem(lax.axis_index("ctx"), 2)
    targets = [(m1_ref, 0), (m1_ref, 1), (m2_ref, 0), (m2_ref, 1), (m3_ref, 0), (m3_ref, 1)]
    targets += [(m4_ref, 0), (own_ref, 0)]
    cross = jnp.zeros((heads, UNIT, E), F32)
    for i, (ref, at) in enumerate(targets):
        kv, qd = keep_ref[2 * i], keep_ref[2 * i + 1]
        kv_got, qd_got = got_ref[2 * i], got_ref[2 * i + 1]
        ref[2 * at * heads : (2 * at + 1) * heads] = kv + kv_got
        ref[(2 * at + 1) * heads : (2 * at + 2) * heads] = qd + qd_got
        cross = cross + jnp.where(core == 0, kv * qd_got, kv_got * qd)
    g_ref[0] = jnp.zeros((UNIT, E), F32)
    g_ref[0, 0:heads] = jnp.sum(cross, axis=1)


def scan_body(chips, heads, x_ref, y_ref, o1_ref, o2_ref, o3_ref, o4_ref, own_ref, g_ref, have, give):
    chip, core, way = place()
    wide, near = 4 * heads, chips // 2
    for ref, go, lane in ((x_ref, way, core), (y_ref, -way, 1 - core)):
        for k in range(1, near):
            at = around(chip, -go * k, chips)
            have[at] = ref[wide * (k - 1) : wide * k].reshape(2, 2 * heads, UNIT, E)
        base = wide * (near - 1)
        have[around(chip, near, chips), lane] = ref[base : base + 2 * heads]
        have[chip, lane] = ref[base + 2 * heads : base + 4 * heads]
    zero = jnp.zeros((2, heads, UNIT, E), F32)
    before, after, cross = zero, zero, zero
    for i in range(chips):
        give[i, :, 0:heads] = before
        cross = cross + before * have[i, :, heads : 2 * heads]
        before = before + have[i, :, 0:heads]
    for i in reversed(range(chips)):
        give[i, :, heads : 2 * heads] = after
        after = after + have[i, :, heads : 2 * heads]
    last = wide * near
    g_ref[...] = x_ref[last : last + 1] + y_ref[last : last + 1]
    g_ref[0, 0:heads] = g_ref[0, 0:heads] + jnp.sum(cross[0] + cross[1], axis=1)
    for k, ref in ((1, o1_ref), (2, o2_ref), (3, o3_ref)):
        ref[0:wide] = give[around(chip, way * k, chips)].reshape(wide, UNIT, E)
        ref[wide : wide + 1] = g_ref[...]
    o4_ref[0 : 2 * heads] = give[around(chip, near, chips), core]
    o4_ref[2 * heads : 2 * heads + 1] = g_ref[...]
    own_ref[...] = give[chip].reshape(wide, UNIT, E)


def beside(*parts):
    return jnp.concatenate(parts, axis=1)


def over(*parts):
    return jnp.concatenate(parts, axis=0)


def intra_body(heads, factor, qs_ref, ks_ref, vs_ref, gy_ref, gain_ref, g_in, dq_ref, dk_ref, dv_ref, g_ref):
    g_ref[...] = g_in[...]
    first = lax.broadcasted_iota(jnp.int32, (CHUNK, CHUNK), 0)
    second = lax.broadcasted_iota(jnp.int32, (CHUNK, CHUNK), 1)
    lower, upper = first >= second, first <= second
    zero = jnp.zeros((E, E), BF16)

    for h in range(heads):
        lanes = slice(h * E, (h + 1) * E)
        at = [slice(i, i + CHUNK) for i in range(0, qs_ref.shape[0], CHUNK)]
        q, k, v, gy = ([ref[some, lanes] for some in at] for ref in (qs_ref, ks_ref, vs_ref, gy_ref))
        count = len(at)
        gain = gain_ref[lanes].reshape(1, E)
        down = jnp.transpose(jnp.broadcast_to(gain, (8, E)))[:, 0:1]
        g_hi, g_lo = halves(down)
        q_t, v_t, gy_t = ([x.T for x in y] for y in (q, v, gy))
        both = [
            mm(beside(v_t[i], gy_t[i]), over(beside(k[i], zero), beside(zero, q[i])), 1, 0)
            for i in range(count)
        ]
        before, after = [None] * count, [None] * count
        for i in range(1, count):
            before[i] = both[i - 1][:, :E] if i == 1 else before[i - 1] + both[i - 1][:, :E]
        for i in reversed(range(count - 1)):
            after[i] = both[i + 1][:, E:] if i == count - 2 else after[i + 1] + both[i + 1][:, E:]
        total = jnp.zeros((1, E), F32)
        for i in range(count):
            left = over(v_t[i] * g_hi, v_t[i] * g_lo)
            if i > 0:
                left = beside(left, over(*halves(before[i] * down)))
            r = mm(beside(gy[i], gy[i]), left, 1, 0)
            w = halves(jnp.where(lower, r[:, :E], 0.0))
            dq = mm(beside(*w), over(k[i], k[i]), 1, 0)
            if i > 0:
                dq += r[:, E:]
            dq_ref[at[i], lanes] = factor * dq
            left = over(*halves(gy_t[i].astype(F32) * down))
            if i + 1 < count:
                left = beside(left, over(*halves(after[i] * down)))
            r = mm(beside(v[i], v[i]), left, 1, 0)
            w = halves(jnp.where(upper, r[:, :E], 0.0))
            dk = mm(beside(*w), over(q[i], q[i]), 1, 0)
            if i + 1 < count:
                dk += r[:, E:]
            dk_ref[at[i], lanes] = factor * dk
            if i + 1 < count:
                left = beside(over(q_t[i], zero), over(*halves(after[i].T)))
                r = mm(beside(k[i], k[i]), left, 1, 0)
            else:
                r = mm(k[i], q_t[i], 1, 0)
            s = halves(jnp.where(upper, r[:, :E], 0.0))
            dv = mm(beside(*s), over(gy[i], gy[i]), 1, 0)
            if i + 1 < count:
                dv += r[:, E:]
            dv = factor * dv
            dv_ref[at[i], lanes] = dv * gain
            total = total + jnp.sum(v[i].astype(F32) * dv, axis=0, keepdims=True)
        g_ref[0, h : h + 1] += total


def slope_body(q_ref, k_ref, v_ref, sq_ref, sk_ref, sv_ref):
    step = 32

    def some_rows(i, carry):
        rows = pl.ds(pl.multiple_of(i * step, step), step)
        for pre, out in ((q_ref, sq_ref), (k_ref, sk_ref), (v_ref, sv_ref)):
            out[rows] = surrogate(pre[0, rows])
        return carry

    lax.fori_loop(0, q_ref.shape[1] // step, some_rows, 0)


def finish_body(
    chips, heads, factor, u_ref, w_ref, own_ref, got_ref, gain_ref, gy_ref, ks_ref, vs_ref,
    dq_ref, dk_ref, dv_ref, sq_ref, sk_ref, sv_ref, oq_ref, ok_ref, ov_ref,
    state, stage, sems,
):
    chip, core, way = place()
    wide, near = 4 * heads, chips // 2
    tiles = wide + 1
    for ref, go, lane in ((u_ref, way, core), (w_ref, -way, 1 - core)):
        for k in range(1, near):
            shard = around(chip, -go * k, chips)
            for b in range(2):
                for t in range(2):
                    base = tiles * (k - 1) + (2 * b + t) * heads
                    state[t, :, rows_of(2 * shard + b)] = ref[base : base + heads]
        for t in range(2):
            base = tiles * (near - 1) + t * heads
            unit = 2 * around(chip, near, chips) + lane
            state[t, :, rows_of(unit)] = ref[base : base + heads]
    for b in range(2):
        for t in range(2):
            base = (2 * b + t) * heads
            state[t, :, rows_of(2 * chip + b)] = own_ref[base : base + heads]
    kind = 1 - core
    mine = unit_list(chip, core, way, chips)
    other = unit_list(chip, 1 - core, -way, chips)
    for i, (here, there) in enumerate(zip(mine, other)):
        state[kind, :, rows_of(here)] += got_ref[2 * i + kind]
        state[kind, :, rows_of(there)] += got_ref[2 * len(mine) + i]
    copies = []
    for h in range(heads):
        lanes = slice(h * E, (h + 1) * E)
        gain = gain_ref[lanes].reshape(1, E)
        gy, k, v = gy_ref[:, lanes], ks_ref[:, lanes], vs_ref[:, lanes]
        m2 = jnp.concatenate(halves(state[0, h] * (gain * factor)), axis=1)
        g_hi, g_lo = halves(state[1, h] * gain)
        dq = dq_ref[:, lanes] + mm(jnp.concatenate([gy, gy], axis=1), m2, 1, 1)
        stage[0, :, lanes] = (dq * sq_ref[:, lanes]).astype(BF16)
        dk = dk_ref[:, lanes] + mm(
            jnp.concatenate([v, v], axis=1), jnp.concatenate([g_hi, g_lo], axis=1), 1, 1
        )
        stage[1, :, lanes] = (dk * sk_ref[:, lanes]).astype(BF16)
        dv = dv_ref[:, lanes] + mm(
            jnp.concatenate([k, k], axis=1), jnp.concatenate([g_hi, g_lo], axis=0), 1, 0
        )
        stage[2, :, lanes] = (dv * sv_ref[:, lanes]).astype(BF16)
        for i, out in enumerate((oq_ref, ok_ref, ov_ref)):
            copy = pltpu.make_async_copy(stage.at[i, :, lanes], out.at[0, :, lanes], sems.at[i, h])
            copy.start()
            copies.append(copy)
    for copy in copies:
        copy.wait()


def pack_body(*refs):
    *parts, out_ref = refs
    base = 0
    for ref in parts:
        out_ref[base : base + ref.shape[0]] = ref[...]
        base += ref.shape[0]


def collect_body(*refs):
    *parts, g_ref, out_ref = refs
    pack_body(*parts, out_ref)
    core = lax.rem(lax.axis_index("ctx"), 2)
    far = g_ref[...] + parts[-1][parts[-1].shape[0] - 1 :]
    total = jnp.where(core == 0, far, 0.0)
    for ref in parts[:-1]:
        total = total + ref[ref.shape[0] - 1 :]
    out_ref[out_ref.shape[0] - 1 :] = total


def params(mib, **more):
    return pltpu.CompilerParams(vmem_limit_bytes=mib * 1024 * 1024, **more)


def cost(us):
    return pl.CostEstimate(flops=int(us * 1e9), bytes_accessed=int(us * 2e6), transcendentals=0)


def per_device(q_count, k_count, v_count, q_pre, k_pre, v_pre, grad_y, gain):
    rows, width = q_count.shape[1], q_count.shape[2]
    heads = width // E
    devices = lax.axis_size("ctx")
    chips = devices // 2
    near = chips // 2
    factor = 1.0 / math.sqrt(E * rows * devices)
    units = E // UNIT
    assert units == devices and near == 4

    def shape(*dims, dtype=F32):
        return jax.ShapeDtypeStruct(dims, dtype)

    def tiles(count):
        return shape(count, UNIT, E)

    swap = [(i, i ^ 1) for i in range(devices)]

    def ring(k):
        pairs = []
        for z in range(chips):
            pairs.append((2 * z, 2 * ((z + k) % chips)))
            pairs.append((2 * z + 1, 2 * ((z - k) % chips) + 1))
        return pairs

    def exchange(parts):
        return [lax.ppermute(part, "ctx", ring(k)) for k, part in enumerate(parts, 1)]

    with jax.named_scope("local_states"):
        keep, send, q_spike, k_spike, v_spike, gy = pl.pallas_call(
            lambda *refs: states_body(chips, heads, factor, *refs),
            in_specs=[pl.BlockSpec(memory_space=pltpu.HBM)] * 4,
            out_shape=[shape(units, heads, UNIT, E), shape(units * 3 // 2, heads, UNIT, E)]
            + [shape(rows, width, dtype=BF16)] * 4,
            scratch_shapes=[
                pltpu.VMEM((3, rows, width), jnp.int32),
                pltpu.VMEM((2, heads, E, E), F32),
                pltpu.SemaphoreType.DMA((4, heads)),
            ],
            compiler_params=params(9),
            cost_estimate=cost(3),
            name="local_states",
        )(*(pltpu.with_memory_space_constraint(x, pltpu.HBM) for x in (q_count, k_count, v_count, grad_y)))
        got = lax.ppermute(send, "ctx", swap)

    with jax.named_scope("chip_states"):
        *parts, own, g_chip = pl.pallas_call(
            lambda *refs: chip_body(chips, heads, *refs),
            out_shape=[tiles(4 * heads)] * 3 + [tiles(2 * heads)] * 2 + [tiles(1)],
            compiler_params=params(2),
            name="chip_states",
        )(keep, got)

    with jax.named_scope("to_owners"):
        parts = exchange(parts)

    with jax.named_scope("intra"):
        gain_late, parts[0] = lax.optimization_barrier((gain, parts[0]))
        dq, dk, dv, g_mine = pl.pallas_call(
            lambda *refs: intra_body(heads, factor, *refs),
            out_shape=[shape(rows, width)] * 3 + [tiles(1)],
            compiler_params=params(4),
            cost_estimate=cost(7),
            name="intra",
        )(q_spike, k_spike, v_spike, gy, gain_late, g_chip)

    with jax.named_scope("to_core"):
        pack = pl.pallas_call(
            pack_body,
            out_shape=tiles(4 * heads * near + 1),
            compiler_params=params(2),
            name="pack",
        )(*parts, own, g_mine)
        pack_got = lax.ppermute(pack, "ctx", swap)

    with jax.named_scope("scan"):
        *parts, own, g_all = pl.pallas_call(
            lambda *refs: scan_body(chips, heads, *refs),
            out_shape=[tiles(4 * heads + 1)] * 3 + [tiles(2 * heads + 1), tiles(4 * heads), tiles(1)],
            scratch_shapes=[pltpu.VMEM((chips, 2, 2 * heads, UNIT, E), F32)] * 2,
            compiler_params=params(4),
            name="scan",
        )(pack, pack_got)

    with jax.named_scope("from_owners"):
        parts = exchange(parts)

    with jax.named_scope("slopes"):
        *late, parts[0] = lax.optimization_barrier((q_pre, k_pre, v_pre, parts[0]))
        sq, sk, sv = pl.pallas_call(
            slope_body,
            out_shape=[shape(rows, width)] * 3,
            compiler_params=params(2),
            cost_estimate=cost(5),
            name="slopes",
        )(*late)

    with jax.named_scope("states"):
        sq, *parts = lax.optimization_barrier((sq, *parts))
        mine = pl.pallas_call(
            collect_body,
            out_shape=tiles((4 * heads + 1) * near - 2 * heads),
            compiler_params=params(2),
            name="collect",
        )(*parts, g_all)
        theirs = lax.ppermute(mine, "ctx", swap)

    with jax.named_scope("grad_gain"):
        g_sum = mine[-1:] + theirs[-1:]
        size = lax.axis_size("dp")
        total = g_sum
        for step in range(1, size):
            total = total + lax.ppermute(
                g_sum, "dp", [(i, (i + step) % size) for i in range(size)]
            )
        grad_gain = total[0, :heads].reshape(width)

    with jax.named_scope("finish"):
        whole = pl.BlockSpec(memory_space=pltpu.VMEM)
        grads = pl.pallas_call(
            lambda *refs: finish_body(chips, heads, factor, *refs),
            in_specs=[whole] * 14,
            out_specs=[pl.BlockSpec(memory_space=pl.ANY)] * 3,
            out_shape=[shape(1, rows, width, dtype=BF16)] * 3,
            scratch_shapes=[
                pltpu.VMEM((2, heads, E, E), F32),
                pltpu.VMEM((3, rows, width), BF16),
                pltpu.SemaphoreType.DMA((3, heads)),
            ],
            compiler_params=params(8),
            name="finish",
        )(mine, theirs, own, got, gain, gy, k_spike, v_spike, dq, dk, dv, sq, sk, sv)
    return (*grads, grad_gain)


def solution(mesh):
    placed = P("dp", "ctx", "head")
    return jax.shard_map(
        per_device,
        mesh=mesh,
        in_specs=(placed,) * 7 + (P("head"),),
        out_specs=(placed,) * 3 + (P("head"),),
        check_vma=False,
    )
```

```python
import math

import jax
import jax.numpy as jnp
from jax import lax
from jax.experimental import pallas as pl
from jax.experimental.pallas import tpu as pltpu
from jax.sharding import PartitionSpec as P

E = 128
SPIKE_STEPS = 4
F32 = jnp.float32
BF16 = jnp.bfloat16
UNIT = 8
CHUNK = 128


def spike(count):
    return ((count.astype(F32) - SPIKE_STEPS / 2) * 0.5).astype(BF16)


def mm(a, b, ca, cb):
    return lax.dot_general(a, b, (((ca,), (cb,)), ((), ())), preferred_element_type=F32)


def halves(x):
    hi = x.astype(BF16)
    return hi, (x - hi.astype(F32)).astype(BF16)


def surrogate(pre):
    w = pre.astype(F32) * (4.0 / math.log(2.0))
    c = jnp.exp2(w) + jnp.exp2(-w)
    b1, b2 = 2.0 * math.cosh(2.0), 2.0 * math.cosh(6.0)
    below = (c + b1) * (c + b2)
    r = pl.reciprocal(below, approx=True)
    r = r * (2.0 - below * r)
    n3 = 2.0 * (b1 + b2)
    n2 = 16.0 + 8.0 * b1 * b2
    n1 = 16.0 * (b1 + b2) + 2.0 * b1 * b2 * (b1 + b2)
    n0 = 8.0 * (b1 * b1 + b2 * b2)
    above = ((n3 * c + n2) * c + n1) * c + n0
    return (above * r) * r


def place():
    me = lax.axis_index("ctx")
    chip, core = me // 2, lax.rem(me, 2)
    return chip, core, 1 - 2 * core


def around(chip, steps, chips):
    return lax.rem(chip + steps + chips, chips)


def unit_list(chip, core, way, chips):
    units = []
    for k in range(1, chips // 2):
        shard = around(chip, way * k, chips)
        units += [2 * shard, 2 * shard + 1]
    return units + [2 * around(chip, chips // 2, chips) + core, 2 * chip + core]


def rows_of(unit):
    return pl.ds(pl.multiple_of(unit * UNIT, UNIT), UNIT)


def states_body(
    chips, heads, factor, q_ref, k_ref, v_ref, gy_ref,
    keep_ref, send_ref, side_ref, qs_ref, ks_ref, vs_ref, gy_out, counts, both, sems,
):
    chip, core, way = place()
    mine = unit_list(chip, core, way, chips)
    other = unit_list(chip, 1 - core, -way, chips)
    copies = []
    for h in range(heads):
        lanes = slice(h * E, (h + 1) * E)
        pairs = [(ref.at[0, :, lanes], counts.at[i, :, lanes]) for i, ref in enumerate((q_ref, k_ref, v_ref))]
        pairs.append((gy_ref.at[0, :, lanes], gy_out.at[:, lanes]))
        copies.append([pltpu.make_async_copy(a, b, sems.at[i, h]) for i, (a, b) in enumerate(pairs)])
        for copy in copies[-1]:
            copy.start()
    for h in range(heads):
        lanes = slice(h * E, (h + 1) * E)
        for copy in copies[h]:
            copy.wait()
        q, k, v = (spike(counts[i, :, lanes]) for i in range(3))
        qs_ref[:, lanes] = q
        ks_ref[:, lanes] = k
        vs_ref[:, lanes] = v
        both[0, h] = mm(k, v, 0, 0)
        both[1, h] = factor * mm(q, gy_out[:, lanes], 0, 0)
    for i, (here, there) in enumerate(zip(mine, other)):
        for t in range(2):
            keep_ref[2 * i + t] = both[t, :, rows_of(here)]
            send_ref[2 * i + t] = both[t, :, rows_of(there)]
        side_ref[i] = both[core, :, rows_of(here)]


def chip_body(chips, heads, keep_ref, got_ref, m1_ref, m2_ref, m3_ref, m4_ref, own_ref, g_ref):
    core = lax.rem(lax.axis_index("ctx"), 2)
    targets = [(m1_ref, 0), (m1_ref, 1), (m2_ref, 0), (m2_ref, 1), (m3_ref, 0), (m3_ref, 1)]
    targets += [(m4_ref, 0), (own_ref, 0)]
    cross = jnp.zeros((heads, UNIT, E), F32)
    for i, (ref, at) in enumerate(targets):
        kv, qd = keep_ref[2 * i], keep_ref[2 * i + 1]
        kv_got, qd_got = got_ref[2 * i], got_ref[2 * i + 1]
        ref[2 * at * heads : (2 * at + 1) * heads] = kv + kv_got
        ref[(2 * at + 1) * heads : (2 * at + 2) * heads] = qd + qd_got
        cross = cross + jnp.where(core == 0, kv * qd_got, kv_got * qd)
    g_ref[0] = jnp.zeros((UNIT, E), F32)
    g_ref[0, 0:heads] = jnp.sum(cross, axis=1)


def scan_body(chips, heads, x_ref, y_ref, o1_ref, o2_ref, o3_ref, o4_ref, own_ref, g_ref, have, give):
    chip, core, way = place()
    wide, near = 4 * heads, chips // 2
    for ref, go, lane in ((x_ref, way, core), (y_ref, -way, 1 - core)):
        for k in range(1, near):
            at = around(chip, -go * k, chips)
            have[at] = ref[wide * (k - 1) : wide * k].reshape(2, 2 * heads, UNIT, E)
        base = wide * (near - 1)
        have[around(chip, near, chips), lane] = ref[base : base + 2 * heads]
        have[chip, lane] = ref[base + 2 * heads : base + 4 * heads]
    zero = jnp.zeros((2, heads, UNIT, E), F32)
    before, after, cross = zero, zero, zero
    for i in range(chips):
        give[i, :, 0:heads] = before
        cross = cross + before * have[i, :, heads : 2 * heads]
        before = before + have[i, :, 0:heads]
    for i in reversed(range(chips)):
        give[i, :, heads : 2 * heads] = after
        after = after + have[i, :, heads : 2 * heads]
    last = wide * near
    g_ref[...] = x_ref[last : last + 1] + y_ref[last : last + 1]
    g_ref[0, 0:heads] = g_ref[0, 0:heads] + jnp.sum(cross[0] + cross[1], axis=1)
    for k, ref in ((1, o1_ref), (2, o2_ref), (3, o3_ref)):
        ref[0:wide] = give[around(chip, way * k, chips)].reshape(wide, UNIT, E)
        ref[wide : wide + 1] = g_ref[...]
    o4_ref[0 : 2 * heads] = give[around(chip, near, chips), core]
    o4_ref[2 * heads : 2 * heads + 1] = g_ref[...]
    own_ref[...] = give[chip].reshape(wide, UNIT, E)


def beside(*parts):
    return jnp.concatenate(parts, axis=1)


def over(*parts):
    return jnp.concatenate(parts, axis=0)


def intra_body(heads, factor, qs_ref, ks_ref, vs_ref, gy_ref, gain_ref, g_in, dq_ref, dk_ref, dv_ref, g_ref):
    g_ref[...] = g_in[...]
    first = lax.broadcasted_iota(jnp.int32, (CHUNK, CHUNK), 0)
    second = lax.broadcasted_iota(jnp.int32, (CHUNK, CHUNK), 1)
    lower, upper = first >= second, first <= second
    zero = jnp.zeros((E, E), BF16)

    for h in range(heads):
        lanes = slice(h * E, (h + 1) * E)
        at = [slice(i, i + CHUNK) for i in range(0, qs_ref.shape[0], CHUNK)]
        q, k, v, gy = ([ref[some, lanes] for some in at] for ref in (qs_ref, ks_ref, vs_ref, gy_ref))
        count = len(at)
        gain = gain_ref[lanes].reshape(1, E)
        down = jnp.transpose(jnp.broadcast_to(gain, (8, E)))[:, 0:1]
        g_hi, g_lo = halves(down)
        q_t, v_t, gy_t = ([x.T for x in y] for y in (q, v, gy))
        both = [
            mm(beside(v_t[i], gy_t[i]), over(beside(k[i], zero), beside(zero, q[i])), 1, 0)
            for i in range(count)
        ]
        before, after = [None] * count, [None] * count
        for i in range(1, count):
            before[i] = both[i - 1][:, :E] if i == 1 else before[i - 1] + both[i - 1][:, :E]
        for i in reversed(range(count - 1)):
            after[i] = both[i + 1][:, E:] if i == count - 2 else after[i + 1] + both[i + 1][:, E:]
        total = jnp.zeros((1, E), F32)
        for i in range(count):
            left = over(v_t[i] * g_hi, v_t[i] * g_lo)
            if i > 0:
                left = beside(left, over(*halves(before[i] * down)))
            r = mm(beside(gy[i], gy[i]), left, 1, 0)
            w = halves(jnp.where(lower, r[:, :E], 0.0))
            dq = mm(beside(*w), over(k[i], k[i]), 1, 0)
            if i > 0:
                dq += r[:, E:]
            dq_ref[at[i], lanes] = factor * dq
            left = over(*halves(gy_t[i].astype(F32) * down))
            if i + 1 < count:
                left = beside(left, over(*halves(after[i] * down)))
            r = mm(beside(v[i], v[i]), left, 1, 0)
            w = halves(jnp.where(upper, r[:, :E], 0.0))
            dk = mm(beside(*w), over(q[i], q[i]), 1, 0)
            if i + 1 < count:
                dk += r[:, E:]
            dk_ref[at[i], lanes] = factor * dk
            if i + 1 < count:
                left = beside(over(q_t[i], zero), over(*halves(after[i].T)))
                r = mm(beside(k[i], k[i]), left, 1, 0)
            else:
                r = mm(k[i], q_t[i], 1, 0)
            s = halves(jnp.where(upper, r[:, :E], 0.0))
            dv = mm(beside(*s), over(gy[i], gy[i]), 1, 0)
            if i + 1 < count:
                dv += r[:, E:]
            dv = factor * dv
            dv_ref[at[i], lanes] = dv * gain
            total = total + jnp.sum(v[i].astype(F32) * dv, axis=0, keepdims=True)
        g_ref[0, h : h + 1] += total


def slope_body(q_ref, k_ref, v_ref, sq_ref, sk_ref, sv_ref):
    step = 32

    def some_rows(i, carry):
        rows = pl.ds(pl.multiple_of(i * step, step), step)
        for pre, out in ((q_ref, sq_ref), (k_ref, sk_ref), (v_ref, sv_ref)):
            out[rows] = surrogate(pre[0, rows])
        return carry

    lax.fori_loop(0, q_ref.shape[1] // step, some_rows, 0)


def finish_body(
    chips, heads, factor, u1_ref, u2_ref, w1_ref, w2_ref, own_ref, got_ref, side_ref, gain_ref, gy_ref, ks_ref, vs_ref,
    dq_ref, dk_ref, dv_ref, sq_ref, sk_ref, sv_ref, oq_ref, ok_ref, ov_ref,
    state, stage, sems,
):
    chip, core, way = place()
    wide, near = 4 * heads, chips // 2
    tiles = wide + 1
    both = ((u1_ref, u2_ref, way, core), (w1_ref, w2_ref, -way, 1 - core))
    for one_ref, two_ref, go, lane in both:
        for k, ref, start in ((1, one_ref, 0), (2, one_ref, tiles), (3, two_ref, 0)):
            shard = around(chip, -go * k, chips)
            for b in range(2):
                for t in range(2):
                    base = start + (2 * b + t) * heads
                    state[t, :, rows_of(2 * shard + b)] = ref[base : base + heads]
        for t in range(2):
            base = tiles + t * heads
            unit = 2 * around(chip, near, chips) + lane
            state[t, :, rows_of(unit)] = two_ref[base : base + heads]
    for b in range(2):
        for t in range(2):
            base = (2 * b + t) * heads
            state[t, :, rows_of(2 * chip + b)] = own_ref[base : base + heads]
    kind = 1 - core
    mine = unit_list(chip, core, way, chips)
    other = unit_list(chip, 1 - core, -way, chips)
    for i, (here, there) in enumerate(zip(mine, other)):
        state[kind, :, rows_of(here)] += got_ref[2 * i + kind]
        state[kind, :, rows_of(there)] += side_ref[i]
    copies = []
    for h in range(heads):
        lanes = slice(h * E, (h + 1) * E)
        gain = gain_ref[lanes].reshape(1, E)
        gy, k, v = gy_ref[:, lanes], ks_ref[:, lanes], vs_ref[:, lanes]
        m2 = jnp.concatenate(halves(state[0, h] * (gain * factor)), axis=1)
        g_hi, g_lo = halves(state[1, h] * gain)
        dq = dq_ref[:, lanes] + mm(jnp.concatenate([gy, gy], axis=1), m2, 1, 1)
        stage[0, :, lanes] = (dq * sq_ref[:, lanes]).astype(BF16)
        dk = dk_ref[:, lanes] + mm(
            jnp.concatenate([v, v], axis=1), jnp.concatenate([g_hi, g_lo], axis=1), 1, 1
        )
        stage[1, :, lanes] = (dk * sk_ref[:, lanes]).astype(BF16)
        dv = dv_ref[:, lanes] + mm(
            jnp.concatenate([k, k], axis=1), jnp.concatenate([g_hi, g_lo], axis=0), 1, 0
        )
        stage[2, :, lanes] = (dv * sv_ref[:, lanes]).astype(BF16)
        for i, out in enumerate((oq_ref, ok_ref, ov_ref)):
            copy = pltpu.make_async_copy(stage.at[i, :, lanes], out.at[0, :, lanes], sems.at[i, h])
            copy.start()
            copies.append(copy)
    for copy in copies:
        copy.wait()


def pack_body(*refs):
    *parts, out_ref = refs
    base = 0
    for ref in parts:
        out_ref[base : base + ref.shape[0]] = ref[...]
        base += ref.shape[0]


def collect_body(first_ref, third_ref, fourth_ref, g_ref, out_ref):
    pack_body(third_ref, fourth_ref, out_ref)
    core = lax.rem(lax.axis_index("ctx"), 2)
    tiles, last = third_ref.shape[0], out_ref.shape[0] - 1
    total = jnp.where(core == 0, g_ref[...] + fourth_ref[last - tiles :], 0.0)
    total = total + first_ref[tiles - 1 : tiles] + first_ref[2 * tiles - 1 :]
    out_ref[last:] = total + third_ref[tiles - 1 :]


def params(mib, **more):
    return pltpu.CompilerParams(vmem_limit_bytes=mib * 1024 * 1024, **more)


def cost(us):
    return pl.CostEstimate(flops=int(us * 1e9), bytes_accessed=int(us * 2e6), transcendentals=0)


def per_device(q_count, k_count, v_count, q_pre, k_pre, v_pre, grad_y, gain):
    rows, width = q_count.shape[1], q_count.shape[2]
    heads = width // E
    devices = lax.axis_size("ctx")
    chips = devices // 2
    near = chips // 2
    factor = 1.0 / math.sqrt(E * rows * devices)
    units = E // UNIT
    assert units == devices and near == 4

    def shape(*dims, dtype=F32):
        return jax.ShapeDtypeStruct(dims, dtype)

    def tiles(count):
        return shape(count, UNIT, E)

    swap = [(i, i ^ 1) for i in range(devices)]

    def ring(k):
        pairs = []
        for z in range(chips):
            pairs.append((2 * z, 2 * ((z + k) % chips)))
            pairs.append((2 * z + 1, 2 * ((z - k) % chips) + 1))
        return pairs

    def exchange(parts):
        return [lax.ppermute(part, "ctx", ring(k)) for k, part in enumerate(parts, 1)]

    with jax.named_scope("local_states"):
        keep, send, side, q_spike, k_spike, v_spike, gy = pl.pallas_call(
            lambda *refs: states_body(chips, heads, factor, *refs),
            in_specs=[pl.BlockSpec(memory_space=pltpu.HBM)] * 4,
            out_shape=[shape(units, heads, UNIT, E)] * 2
            + [shape(units // 2, heads, UNIT, E)]
            + [shape(rows, width, dtype=BF16)] * 4,
            scratch_shapes=[
                pltpu.VMEM((3, rows, width), jnp.int32),
                pltpu.VMEM((2, heads, E, E), F32),
                pltpu.SemaphoreType.DMA((4, heads)),
            ],
            compiler_params=params(9),
            cost_estimate=cost(3),
            name="local_states",
        )(*(pltpu.with_memory_space_constraint(x, pltpu.HBM) for x in (q_count, k_count, v_count, grad_y)))
        got = lax.ppermute(send, "ctx", swap)

    with jax.named_scope("chip_states"):
        *parts, own, g_chip = pl.pallas_call(
            lambda *refs: chip_body(chips, heads, *refs),
            out_shape=[tiles(4 * heads)] * 3 + [tiles(2 * heads)] * 2 + [tiles(1)],
            compiler_params=params(2),
            name="chip_states",
        )(keep, got)

    with jax.named_scope("to_owners"):
        side, g_chip = lax.optimization_barrier((side, g_chip))
        parts = exchange(parts)
        side_got = lax.ppermute(side, "ctx", swap)

    with jax.named_scope("intra"):
        gain_late, parts[0] = lax.optimization_barrier((gain, parts[0]))
        dq, dk, dv, g_mine = pl.pallas_call(
            lambda *refs: intra_body(heads, factor, *refs),
            out_shape=[shape(rows, width)] * 3 + [tiles(1)],
            compiler_params=params(4),
            cost_estimate=cost(7),
            name="intra",
        )(q_spike, k_spike, v_spike, gy, gain_late, g_chip)

    with jax.named_scope("to_core"):
        side_got, g_mine = lax.optimization_barrier((side_got, g_mine))
        pack = pl.pallas_call(
            pack_body,
            out_shape=tiles(4 * heads * near + 1),
            compiler_params=params(2),
            name="pack",
        )(*parts, own, g_mine)
        pack_got = lax.ppermute(pack, "ctx", swap)

    with jax.named_scope("scan"):
        *parts, own, g_all = pl.pallas_call(
            lambda *refs: scan_body(chips, heads, *refs),
            out_shape=[tiles(4 * heads + 1)] * 3 + [tiles(2 * heads + 1), tiles(4 * heads), tiles(1)],
            scratch_shapes=[pltpu.VMEM((chips, 2, 2 * heads, UNIT, E), F32)] * 2,
            compiler_params=params(4),
            name="scan",
        )(pack, pack_got)

    with jax.named_scope("from_owners"):
        parts = exchange(parts)

    with jax.named_scope("first_states"):
        first = pl.pallas_call(
            pack_body, out_shape=tiles(8 * heads + 2), compiler_params=params(2), name="collect_first"
        )(parts[0], parts[1])
        first_got = lax.ppermute(first, "ctx", swap)

    with jax.named_scope("slopes"):
        *late, first = lax.optimization_barrier((q_pre, k_pre, v_pre, first))
        sq, sk, sv = pl.pallas_call(
            slope_body,
            out_shape=[shape(rows, width)] * 3,
            compiler_params=params(2),
            cost_estimate=cost(5),
            name="slopes",
        )(*late)

    with jax.named_scope("states"):
        sq, *parts = lax.optimization_barrier((sq, *parts))
        second = pl.pallas_call(
            collect_body,
            out_shape=tiles(6 * heads + 2),
            compiler_params=params(2),
            name="collect_second",
        )(first, parts[2], parts[3], g_all)
        second_got = lax.ppermute(second, "ctx", swap)
        first_got, second_got = lax.optimization_barrier((first_got, second_got))

    with jax.named_scope("grad_gain"):
        g_sum = second[-1:] + second_got[-1:]
        size = lax.axis_size("dp")
        total = g_sum
        for step in range(1, size):
            total = total + lax.ppermute(
                g_sum, "dp", [(i, (i + step) % size) for i in range(size)]
            )
        grad_gain = total[0, :heads].reshape(width)

    with jax.named_scope("finish"):
        whole = pl.BlockSpec(memory_space=pltpu.VMEM)
        grads = pl.pallas_call(
            lambda *refs: finish_body(chips, heads, factor, *refs),
            in_specs=[whole] * 17,
            out_specs=[pl.BlockSpec(memory_space=pl.ANY)] * 3,
            out_shape=[shape(1, rows, width, dtype=BF16)] * 3,
            scratch_shapes=[
                pltpu.VMEM((2, heads, E, E), F32),
                pltpu.VMEM((3, rows, width), BF16),
                pltpu.SemaphoreType.DMA((3, heads)),
            ],
            compiler_params=params(8),
            name="finish",
        )(first, second, first_got, second_got, own, got, side_got, gain, gy, k_spike, v_spike, dq, dk, dv, sq, sk, sv)
    return (*grads, grad_gain)


def solution(mesh):
    placed = P("dp", "ctx", "head")
    return jax.shard_map(
        per_device,
        mesh=mesh,
        in_specs=(placed,) * 7 + (P("head"),),
        out_specs=(placed,) * 3 + (P("head"),),
        check_vma=False,
    )
```

```python
import math

import jax
import jax.numpy as jnp
from jax import lax
from jax.experimental import pallas as pl
from jax.experimental.pallas import tpu as pltpu
from jax.sharding import PartitionSpec as P

E = 128
SPIKE_STEPS = 4
F32 = jnp.float32
BF16 = jnp.bfloat16
UNIT = 8
CHUNK = 128


def spike(count):
    return ((count.astype(F32) - SPIKE_STEPS / 2) * 0.5).astype(BF16)


def mm(a, b, ca, cb):
    return lax.dot_general(a, b, (((ca,), (cb,)), ((), ())), preferred_element_type=F32)


def halves(x):
    hi = x.astype(BF16)
    return hi, (x - hi.astype(F32)).astype(BF16)


def surrogate(pre):
    w = pre.astype(F32) * (4.0 / math.log(2.0))
    c = jnp.exp2(w) + jnp.exp2(-w)
    b1, b2 = 2.0 * math.cosh(2.0), 2.0 * math.cosh(6.0)
    below = (c + b1) * (c + b2)
    r = pl.reciprocal(below, approx=True)
    r = r * (2.0 - below * r)
    n3 = 2.0 * (b1 + b2)
    n2 = 16.0 + 8.0 * b1 * b2
    n1 = 16.0 * (b1 + b2) + 2.0 * b1 * b2 * (b1 + b2)
    n0 = 8.0 * (b1 * b1 + b2 * b2)
    above = ((n3 * c + n2) * c + n1) * c + n0
    return (above * r) * r


def place():
    me = lax.axis_index("ctx")
    chip, core = me // 2, lax.rem(me, 2)
    return chip, core, 1 - 2 * core


def around(chip, steps, chips):
    return lax.rem(chip + steps + chips, chips)


def unit_list(chip, core, way, chips):
    units = []
    for k in range(1, chips // 2):
        shard = around(chip, way * k, chips)
        units += [2 * shard, 2 * shard + 1]
    return units + [2 * around(chip, chips // 2, chips) + core, 2 * chip + core]


def rows_of(unit):
    return pl.ds(pl.multiple_of(unit * UNIT, UNIT), UNIT)


def states_body(
    chips, heads, factor, q_ref, k_ref, v_ref, gy_ref,
    keep_ref, send_ref, side_ref, qs_ref, ks_ref, vs_ref, gy_out, counts, both, sems,
):
    chip, core, way = place()
    mine = unit_list(chip, core, way, chips)
    other = unit_list(chip, 1 - core, -way, chips)
    copies = []
    for h in range(heads):
        lanes = slice(h * E, (h + 1) * E)
        pairs = [(ref.at[0, :, lanes], counts.at[i, :, lanes]) for i, ref in enumerate((q_ref, k_ref, v_ref))]
        pairs.append((gy_ref.at[0, :, lanes], gy_out.at[:, lanes]))
        copies.append([pltpu.make_async_copy(a, b, sems.at[i, h]) for i, (a, b) in enumerate(pairs)])
        for copy in copies[-1]:
            copy.start()
    for h in range(heads):
        lanes = slice(h * E, (h + 1) * E)
        for copy in copies[h]:
            copy.wait()
        q, k, v = (spike(counts[i, :, lanes]) for i in range(3))
        qs_ref[:, lanes] = q
        ks_ref[:, lanes] = k
        vs_ref[:, lanes] = v
        both[0, h] = mm(k, v, 0, 0)
        both[1, h] = factor * mm(q, gy_out[:, lanes], 0, 0)
    for i, (here, there) in enumerate(zip(mine, other)):
        for t in range(2):
            keep_ref[2 * i + t] = both[t, :, rows_of(here)]
            send_ref[2 * i + t] = both[t, :, rows_of(there)]
        side_ref[i] = both[core, :, rows_of(here)]


def chip_body(chips, heads, keep_ref, got_ref, m1_ref, m2_ref, m3_ref, m4_ref, own_ref, g_ref):
    core = lax.rem(lax.axis_index("ctx"), 2)
    targets = [(m1_ref, 0), (m1_ref, 1), (m2_ref, 0), (m2_ref, 1), (m3_ref, 0), (m3_ref, 1)]
    targets += [(m4_ref, 0), (own_ref, 0)]
    cross = jnp.zeros((heads, UNIT, E), F32)
    for i, (ref, at) in enumerate(targets):
        kv, qd = keep_ref[2 * i], keep_ref[2 * i + 1]
        kv_got, qd_got = got_ref[2 * i], got_ref[2 * i + 1]
        ref[2 * at * heads : (2 * at + 1) * heads] = kv + kv_got
        ref[(2 * at + 1) * heads : (2 * at + 2) * heads] = qd + qd_got
        cross = cross + jnp.where(core == 0, kv * qd_got, kv_got * qd)
    g_ref[0] = jnp.zeros((UNIT, E), F32)
    g_ref[0, 0:heads] = jnp.sum(cross, axis=1)


def scan_body(chips, heads, x1_ref, x2_ref, y1_ref, y2_ref, o1_ref, o2_ref, o3_ref, o4_ref, own_ref, g_ref, have, give):
    chip, core, way = place()
    wide, near = 4 * heads, chips // 2
    both = ((x1_ref, x2_ref, way, core), (y1_ref, y2_ref, -way, 1 - core))
    for one_ref, two_ref, go, lane in both:
        for k, ref, base in ((1, one_ref, 0), (2, one_ref, wide), (3, two_ref, 0)):
            at = around(chip, -go * k, chips)
            have[at] = ref[base : base + wide].reshape(2, 2 * heads, UNIT, E)
        have[chip, lane] = one_ref[2 * wide :]
        have[around(chip, near, chips), lane] = two_ref[wide : wide + 2 * heads]
    zero = jnp.zeros((2, heads, UNIT, E), F32)
    before, after, cross = zero, zero, zero
    for i in range(chips):
        give[i, :, 0:heads] = before
        cross = cross + before * have[i, :, heads : 2 * heads]
        before = before + have[i, :, 0:heads]
    for i in reversed(range(chips)):
        give[i, :, heads : 2 * heads] = after
        after = after + have[i, :, heads : 2 * heads]
    last = wide + 2 * heads
    g_ref[...] = x2_ref[last:] + y2_ref[last:]
    g_ref[0, 0:heads] = g_ref[0, 0:heads] + jnp.sum(cross[0] + cross[1], axis=1)
    for k, ref in ((1, o1_ref), (2, o2_ref), (3, o3_ref)):
        ref[0:wide] = give[around(chip, way * k, chips)].reshape(wide, UNIT, E)
        ref[wide : wide + 1] = g_ref[...]
    o4_ref[0 : 2 * heads] = give[around(chip, near, chips), core]
    o4_ref[2 * heads : 2 * heads + 1] = g_ref[...]
    own_ref[...] = give[chip].reshape(wide, UNIT, E)


def beside(*parts):
    return jnp.concatenate(parts, axis=1)


def over(*parts):
    return jnp.concatenate(parts, axis=0)


def intra_body(heads, factor, qs_ref, ks_ref, vs_ref, gy_ref, gain_ref, g_in, dq_ref, dk_ref, dv_ref, g_ref):
    g_ref[...] = g_in[...]
    first = lax.broadcasted_iota(jnp.int32, (CHUNK, CHUNK), 0)
    second = lax.broadcasted_iota(jnp.int32, (CHUNK, CHUNK), 1)
    lower, upper = first >= second, first <= second
    zero = jnp.zeros((E, E), BF16)

    for h in range(heads):
        lanes = slice(h * E, (h + 1) * E)
        at = [slice(i, i + CHUNK) for i in range(0, qs_ref.shape[0], CHUNK)]
        q, k, v, gy = ([ref[some, lanes] for some in at] for ref in (qs_ref, ks_ref, vs_ref, gy_ref))
        count = len(at)
        gain = gain_ref[lanes].reshape(1, E)
        down = jnp.transpose(jnp.broadcast_to(gain, (8, E)))[:, 0:1]
        g_hi, g_lo = halves(down)
        q_t, v_t, gy_t = ([x.T for x in y] for y in (q, v, gy))
        both = [
            mm(beside(v_t[i], gy_t[i]), over(beside(k[i], zero), beside(zero, q[i])), 1, 0)
            for i in range(count)
        ]
        before, after = [None] * count, [None] * count
        for i in range(1, count):
            before[i] = both[i - 1][:, :E] if i == 1 else before[i - 1] + both[i - 1][:, :E]
        for i in reversed(range(count - 1)):
            after[i] = both[i + 1][:, E:] if i == count - 2 else after[i + 1] + both[i + 1][:, E:]
        total = jnp.zeros((1, E), F32)
        for i in range(count):
            left = over(v_t[i] * g_hi, v_t[i] * g_lo)
            if i > 0:
                left = beside(left, over(*halves(before[i] * down)))
            r = mm(beside(gy[i], gy[i]), left, 1, 0)
            w = halves(jnp.where(lower, r[:, :E], 0.0))
            dq = mm(beside(*w), over(k[i], k[i]), 1, 0)
            if i > 0:
                dq += r[:, E:]
            dq_ref[at[i], lanes] = factor * dq
            left = over(*halves(gy_t[i].astype(F32) * down))
            if i + 1 < count:
                left = beside(left, over(*halves(after[i] * down)))
            r = mm(beside(v[i], v[i]), left, 1, 0)
            w = halves(jnp.where(upper, r[:, :E], 0.0))
            dk = mm(beside(*w), over(q[i], q[i]), 1, 0)
            if i + 1 < count:
                dk += r[:, E:]
            dk_ref[at[i], lanes] = factor * dk
            if i + 1 < count:
                left = beside(over(q_t[i], zero), over(*halves(after[i].T)))
                r = mm(beside(k[i], k[i]), left, 1, 0)
            else:
                r = mm(k[i], q_t[i], 1, 0)
            s = halves(jnp.where(upper, r[:, :E], 0.0))
            dv = mm(beside(*s), over(gy[i], gy[i]), 1, 0)
            if i + 1 < count:
                dv += r[:, E:]
            dv = factor * dv
            dv_ref[at[i], lanes] = dv * gain
            total = total + jnp.sum(v[i].astype(F32) * dv, axis=0, keepdims=True)
        g_ref[0, h : h + 1] += total


def slope_body(q_ref, k_ref, v_ref, sq_ref, sk_ref, sv_ref):
    step = 32

    def some_rows(i, carry):
        rows = pl.ds(pl.multiple_of(i * step, step), step)
        for pre, out in ((q_ref, sq_ref), (k_ref, sk_ref), (v_ref, sv_ref)):
            out[rows] = surrogate(pre[0, rows])
        return carry

    lax.fori_loop(0, q_ref.shape[1] // step, some_rows, 0)


def finish_body(
    chips, heads, factor, u1_ref, u2_ref, w1_ref, w2_ref, own_ref, got_ref, side_ref, gain_ref, gy_ref, ks_ref, vs_ref,
    dq_ref, dk_ref, dv_ref, sq_ref, sk_ref, sv_ref, oq_ref, ok_ref, ov_ref,
    state, stage, sems,
):
    chip, core, way = place()
    wide, near = 4 * heads, chips // 2
    tiles = wide + 1
    both = ((u1_ref, u2_ref, way, core), (w1_ref, w2_ref, -way, 1 - core))
    for one_ref, two_ref, go, lane in both:
        for k, ref, start in ((1, one_ref, 0), (2, one_ref, tiles), (3, two_ref, 0)):
            shard = around(chip, -go * k, chips)
            for b in range(2):
                for t in range(2):
                    base = start + (2 * b + t) * heads
                    state[t, :, rows_of(2 * shard + b)] = ref[base : base + heads]
        for t in range(2):
            base = tiles + t * heads
            unit = 2 * around(chip, near, chips) + lane
            state[t, :, rows_of(unit)] = two_ref[base : base + heads]
    for b in range(2):
        for t in range(2):
            base = (2 * b + t) * heads
            state[t, :, rows_of(2 * chip + b)] = own_ref[base : base + heads]
    kind = 1 - core
    mine = unit_list(chip, core, way, chips)
    other = unit_list(chip, 1 - core, -way, chips)
    for i, (here, there) in enumerate(zip(mine, other)):
        state[kind, :, rows_of(here)] += got_ref[2 * i + kind]
        state[kind, :, rows_of(there)] += side_ref[i]
    copies = []
    for h in range(heads):
        lanes = slice(h * E, (h + 1) * E)
        gain = gain_ref[lanes].reshape(1, E)
        gy, k, v = gy_ref[:, lanes], ks_ref[:, lanes], vs_ref[:, lanes]
        m2 = jnp.concatenate(halves(state[0, h] * (gain * factor)), axis=1)
        g_hi, g_lo = halves(state[1, h] * gain)
        dq = dq_ref[:, lanes] + mm(jnp.concatenate([gy, gy], axis=1), m2, 1, 1)
        stage[0, :, lanes] = (dq * sq_ref[:, lanes]).astype(BF16)
        dk = dk_ref[:, lanes] + mm(
            jnp.concatenate([v, v], axis=1), jnp.concatenate([g_hi, g_lo], axis=1), 1, 1
        )
        stage[1, :, lanes] = (dk * sk_ref[:, lanes]).astype(BF16)
        dv = dv_ref[:, lanes] + mm(
            jnp.concatenate([k, k], axis=1), jnp.concatenate([g_hi, g_lo], axis=0), 1, 0
        )
        stage[2, :, lanes] = (dv * sv_ref[:, lanes]).astype(BF16)
        for i, out in enumerate((oq_ref, ok_ref, ov_ref)):
            copy = pltpu.make_async_copy(stage.at[i, :, lanes], out.at[0, :, lanes], sems.at[i, h])
            copy.start()
            copies.append(copy)
    for copy in copies:
        copy.wait()


def pack_body(*refs):
    *parts, out_ref = refs
    base = 0
    for ref in parts:
        out_ref[base : base + ref.shape[0]] = ref[...]
        base += ref.shape[0]


def collect_body(first_ref, third_ref, fourth_ref, g_ref, out_ref):
    pack_body(third_ref, fourth_ref, out_ref)
    core = lax.rem(lax.axis_index("ctx"), 2)
    tiles, last = third_ref.shape[0], out_ref.shape[0] - 1
    total = jnp.where(core == 0, g_ref[...] + fourth_ref[last - tiles :], 0.0)
    total = total + first_ref[tiles - 1 : tiles] + first_ref[2 * tiles - 1 :]
    out_ref[last:] = total + third_ref[tiles - 1 :]


def params(mib, **more):
    return pltpu.CompilerParams(vmem_limit_bytes=mib * 1024 * 1024, **more)


def cost(us):
    return pl.CostEstimate(flops=int(us * 1e9), bytes_accessed=int(us * 2e6), transcendentals=0)


def per_device(q_count, k_count, v_count, q_pre, k_pre, v_pre, grad_y, gain):
    rows, width = q_count.shape[1], q_count.shape[2]
    heads = width // E
    devices = lax.axis_size("ctx")
    chips = devices // 2
    near = chips // 2
    factor = 1.0 / math.sqrt(E * rows * devices)
    units = E // UNIT
    assert units == devices and near == 4

    def shape(*dims, dtype=F32):
        return jax.ShapeDtypeStruct(dims, dtype)

    def tiles(count):
        return shape(count, UNIT, E)

    swap = [(i, i ^ 1) for i in range(devices)]

    def ring(k):
        pairs = []
        for z in range(chips):
            pairs.append((2 * z, 2 * ((z + k) % chips)))
            pairs.append((2 * z + 1, 2 * ((z - k) % chips) + 1))
        return pairs

    def exchange(parts):
        return [lax.ppermute(part, "ctx", ring(k)) for k, part in enumerate(parts, 1)]

    with jax.named_scope("local_states"):
        keep, send, side, q_spike, k_spike, v_spike, gy = pl.pallas_call(
            lambda *refs: states_body(chips, heads, factor, *refs),
            in_specs=[pl.BlockSpec(memory_space=pltpu.HBM)] * 4,
            out_shape=[shape(units, heads, UNIT, E)] * 2
            + [shape(units // 2, heads, UNIT, E)]
            + [shape(rows, width, dtype=BF16)] * 4,
            scratch_shapes=[
                pltpu.VMEM((3, rows, width), jnp.int32),
                pltpu.VMEM((2, heads, E, E), F32),
                pltpu.SemaphoreType.DMA((4, heads)),
            ],
            compiler_params=params(9),
            cost_estimate=cost(3),
            name="local_states",
        )(*(pltpu.with_memory_space_constraint(x, pltpu.HBM) for x in (q_count, k_count, v_count, grad_y)))
        got = lax.ppermute(send, "ctx", swap)

    with jax.named_scope("chip_states"):
        *parts, own, g_chip = pl.pallas_call(
            lambda *refs: chip_body(chips, heads, *refs),
            out_shape=[tiles(4 * heads)] * 3 + [tiles(2 * heads)] * 2 + [tiles(1)],
            compiler_params=params(2),
            name="chip_states",
        )(keep, got)

    with jax.named_scope("to_owners"):
        parts = exchange(parts)

    with jax.named_scope("intra"):
        gain_late, parts[0] = lax.optimization_barrier((gain, parts[0]))
        dq, dk, dv, g_mine = pl.pallas_call(
            lambda *refs: intra_body(heads, factor, *refs),
            out_shape=[shape(rows, width)] * 3 + [tiles(1)],
            compiler_params=params(4),
            cost_estimate=cost(7),
            name="intra",
        )(q_spike, k_spike, v_spike, gy, gain_late, g_chip)

    with jax.named_scope("to_core"):
        first = pl.pallas_call(
            pack_body, out_shape=tiles(10 * heads), compiler_params=params(2), name="pack_first"
        )(parts[0], parts[1], own)
        first_got = lax.ppermute(first, "ctx", swap)
        second = pl.pallas_call(
            pack_body, out_shape=tiles(6 * heads + 1), compiler_params=params(2), name="pack_second"
        )(parts[2], parts[3], g_mine)
        second_got = lax.ppermute(second, "ctx", swap)

    with jax.named_scope("scan"):
        *parts, own, g_all = pl.pallas_call(
            lambda *refs: scan_body(chips, heads, *refs),
            out_shape=[tiles(4 * heads + 1)] * 3 + [tiles(2 * heads + 1), tiles(4 * heads), tiles(1)],
            scratch_shapes=[pltpu.VMEM((chips, 2, 2 * heads, UNIT, E), F32)] * 2,
            compiler_params=params(4),
            name="scan",
        )(first, second, first_got, second_got)

    with jax.named_scope("from_owners"):
        parts = exchange(parts)

    with jax.named_scope("side_states"):
        side, g_all = lax.optimization_barrier((side, g_all))
        side_got = lax.ppermute(side, "ctx", swap)

    with jax.named_scope("first_states"):
        first = pl.pallas_call(
            pack_body, out_shape=tiles(8 * heads + 2), compiler_params=params(2), name="collect_first"
        )(parts[0], parts[1])
        first_got = lax.ppermute(first, "ctx", swap)

    with jax.named_scope("slopes"):
        *late, first = lax.optimization_barrier((q_pre, k_pre, v_pre, first))
        sq, sk, sv = pl.pallas_call(
            slope_body,
            out_shape=[shape(rows, width)] * 3,
            compiler_params=params(2),
            cost_estimate=cost(5),
            name="slopes",
        )(*late)

    with jax.named_scope("states"):
        sq, side_got, *parts = lax.optimization_barrier((sq, side_got, *parts))
        second = pl.pallas_call(
            collect_body,
            out_shape=tiles(6 * heads + 2),
            compiler_params=params(2),
            name="collect_second",
        )(first, parts[2], parts[3], g_all)
        second_got = lax.ppermute(second, "ctx", swap)
        first_got, second_got = lax.optimization_barrier((first_got, second_got))

    with jax.named_scope("grad_gain"):
        g_sum = second[-1:] + second_got[-1:]
        size = lax.axis_size("dp")
        total = g_sum
        for step in range(1, size):
            total = total + lax.ppermute(
                g_sum, "dp", [(i, (i + step) % size) for i in range(size)]
            )
        grad_gain = total[0, :heads].reshape(width)

    with jax.named_scope("finish"):
        whole = pl.BlockSpec(memory_space=pltpu.VMEM)
        grads = pl.pallas_call(
            lambda *refs: finish_body(chips, heads, factor, *refs),
            in_specs=[whole] * 17,
            out_specs=[pl.BlockSpec(memory_space=pl.ANY)] * 3,
            out_shape=[shape(1, rows, width, dtype=BF16)] * 3,
            scratch_shapes=[
                pltpu.VMEM((2, heads, E, E), F32),
                pltpu.VMEM((3, rows, width), BF16),
                pltpu.SemaphoreType.DMA((3, heads)),
            ],
            compiler_params=params(8),
            name="finish",
        )(first, second, first_got, second_got, own, got, side_got, gain, gy, k_spike, v_spike, dq, dk, dv, sq, sk, sv)
    return (*grads, grad_gain)


def solution(mesh):
    placed = P("dp", "ctx", "head")
    return jax.shard_map(
        per_device,
        mesh=mesh,
        in_specs=(placed,) * 7 + (P("head"),),
        out_specs=(placed,) * 3 + (P("head"),),
        check_vma=False,
    )
```
